32 devices in a mesh: cls: 4 (over z), dom: 8 (over y, x, core).
Axes of the slice: x: 2, y: 2, z: 4, core: 2. Of those that a mesh axis runs over, the one named last changes fastest.
Arguments:
- particles: bfloat16 [4096, 8192], P(('cls', 'dom')), may hold values from -6 to 6
- assign: int32 [4096, 1], P(('cls', 'dom')), may hold values from 0 to 7; in each aligned block of 128 rows (0 to 127, 128 to 255, ...) at most 16 rows name the same one
- inv_sigma: bfloat16 [4096], P(('cls', 'dom')), may hold values from 0.5 to 300, as said below
- projections: bfloat16 [8, 16, 8192], P('cls', 'dom'), may hold values from -0.0625 to 0.0625
Outputs:
- class_sums: float32 [8, 16, 8192], P('cls', 'dom')
- evidence: float32 [4096], P(('cls', 'dom'))
The draws below stay inside these ranges and needn't reach their ends.
Inputs may be any that keep to these rules, and one draw needn't show every extreme that they name: `assign`: among the 128 particles of one device (aligned blocks of rows) no class is named more than 16 times, a bound that some block reaches. `inv_sigma`: each particle's noise precision, positive.
All inputs are finite; a program needn't handle non-finite values.
Results may differ from the reference program's by a relative error of at most 0.0023.
Values may be sent and summed in bfloat16 or wider, within the bound.
No kernel may reach another device: no remote copies, remote signals or barrier semaphores. Data moves between devices by JAX's collectives and lax.ppermute only.
A program may use at most 64 MiB of HBM per device.

```python
import math
import jax
import jax.numpy as jnp
import numpy as np
from jax import lax

F = 8192
PART_DEV = 128
K = 8
R = 16
CAP = 16
PARTICLES = 4096
N_CLS = 4
N_DOM = 8


def draw_inv_sigma(key, part):
    lower, upper = (0.5, 16.0)
    fraction = jax.random.uniform(key, (PARTICLES,), jnp.float32)
    values = jnp.exp(math.log(lower) + fraction * (math.log(upper) - math.log(lower)))
    return values.astype(jnp.bfloat16)


def steps_of(stream_key, shape, split, smallest, high):
    level = 1.0
    for position, parts in split:
        draws = jax.random.uniform(jax.random.fold_in(jax.random.fold_in(stream_key, 6), position), (parts,), jnp.float32, smallest / len(split), high / len(split))
        level = level * jnp.repeat(jnp.exp(draws), shape[position] // parts).reshape((-1,) + (1,) * (len(shape) - 1 - position))
    return level


def assign_block(key, own, number, rows, number_of, top, limit, slope):
    ranking = jax.random.permutation(key, number_of)
    crowded, ordinary = load_shares(number_of, rows * top, limit, slope, True), load_shares(number_of, rows * top, limit, slope, False)
    places = jnp.arange(number_of)

    def named(sizes, turn):
        used = int((sizes > 0).sum())
        fixed = max(1, used // 4)
        moved = fixed + (places - fixed + turn * (used - fixed)) % max(1, number_of - fixed)
        return jnp.zeros((number_of,), jnp.int32).at[ranking[jnp.where(places < fixed, places, moved)]].set(jnp.asarray(sizes, jnp.int32))

    sizes = jnp.where(number % 4 == 0, named(crowded, number // 4), named(ordinary, number - number // 4 - 1))
    mixed = jax.random.permutation(jax.random.fold_in(own, 3), number_of)
    giver, receiver = mixed[0:number_of // 2 * 2:2], mixed[1:number_of // 2 * 2:2]
    margin = jnp.minimum(sizes[giver] - 1, limit - sizes[receiver]) // 2
    margin = jnp.where((giver == ranking[0]) | (receiver == ranking[0]) | (sizes[receiver] == 0), 0, jnp.maximum(margin, 0))
    moved = jax.random.randint(jax.random.fold_in(own, 4), (number_of // 2,), 0, 1 << 20) % (margin + 1)
    sizes = sizes.at[giver].add(-moved).at[receiver].add(moved)
    labels = jnp.searchsorted(jnp.cumsum(sizes), jnp.arange(rows * top), side="right").astype(jnp.int32)
    listing = labels.reshape(top, rows).T
    listing = listing[jax.random.permutation(jax.random.fold_in(own, 1), rows)]
    turn = jax.random.randint(jax.random.fold_in(own, 2), (rows, 1), 0, top)
    return jnp.take_along_axis(listing, (jnp.arange(top)[None, :] + turn) % top, axis=1)


def load_shares(amount, total, limit, lean, full):
    loads = [(1 << 20) // math.isqrt(rank ** lean) + 1 for rank in range(1, amount + 1)]
    largest = limit if full else min(limit, max(-(-total // amount), total * loads[0] // sum(loads)))
    least = 1 if total - largest >= amount - 1 else 0
    holding, surplus = [largest] + [least] * (amount - 1), total - largest - least * (amount - 1)
    while surplus > 0:
        candidates = [i for i in range(1, amount) if holding[i] < largest] or [i for i in range(1, amount) if holding[i] < limit]
        mass, left = sum([loads[i] for i in candidates]), surplus
        for i in candidates:
            extra = min(limit - holding[i], max(1, left * loads[i] // mass), surplus)
            holding[i] = holding[i] + extra
            surplus = surplus - extra
    return np.array(holding)


def bell_draw(stream_key, dims, scale, bound, shards=(), kind=jnp.bfloat16):
    level = steps_of(stream_key, dims, shards, -0.22, 0.18) if shards else 1.0
    values = jax.random.normal(stream_key, dims, jnp.float32) * scale * level
    return jnp.minimum(jnp.maximum(values, -bound), bound).astype(kind)


def setup_inputs(seed: int = 0) -> dict:
    keys = jax.random.split(jax.random.key(seed), 5)
    particles = bell_draw(keys[0], (PARTICLES, F), 1.0, 6.0, ((0, 32),))
    assign_keys = jax.random.split(jax.random.fold_in(keys[1], 1), PARTICLES // PART_DEV)
    assign_turns = jax.random.permutation(jax.random.fold_in(keys[1], 3), PARTICLES // PART_DEV)
    assign = jax.vmap(lambda own, number: assign_block(jax.random.fold_in(keys[1], 2), own, number, PART_DEV, K, 1, CAP, 1))(assign_keys, assign_turns).reshape((PARTICLES, 1))
    inv_sigma = draw_inv_sigma(jax.random.fold_in(keys[4], 71), 0)
    projections = bell_draw(keys[3], (K, R, F), F ** -0.5, 0.0625, ((0, 4), (1, 8)))
    return {"particles": particles, "assign": assign, "inv_sigma": inv_sigma, "projections": projections}


def reference(particles, assign, inv_sigma, projections):
    classes = projections.shape[0]
    most_rows = N_CLS * N_DOM * CAP
    total = particles.shape[0]
    class_id = assign[:, 0]
    halves = 0.5 * jnp.sum(jnp.square(projections.astype(jnp.float32)), axis=2)

    def single(klass):
        index_list = jnp.nonzero(class_id == klass, size=most_rows, fill_value=total)[0].astype(jnp.int32)
        is_live = index_list < total
        safe_index = jnp.minimum(index_list, total - 1)
        picked = particles[safe_index]
        precision = jnp.where(is_live, inv_sigma[safe_index].astype(jnp.float32), 0.0)
        project = lax.dynamic_index_in_dim(projections, klass, 0, keepdims=False)
        class_half = lax.dynamic_index_in_dim(halves, klass, 0, keepdims=False)
        products = jnp.dot(picked, project.T, preferred_element_type=jnp.float32)
        scores = precision[:, None] * (products - class_half[None, :])
        largest = jnp.max(scores, axis=1, keepdims=True)
        exponent = jnp.exp(scores - largest)
        totals = jnp.sum(exponent, axis=1, keepdims=True)
        weights = jnp.where(is_live[:, None], exponent / totals, 0.0).astype(jnp.bfloat16)
        sums = lax.dot_general(weights, picked, (((0,), (0,)), ((), ())), preferred_element_type=jnp.float32)
        log_total = largest[:, 0] + jnp.log(totals[:, 0])
        return sums, log_total, index_list

    sums, log_total, index_list = lax.map(single, jnp.arange(classes, dtype=jnp.int32))
    evidence = jnp.zeros((total,), jnp.float32).at[index_list.reshape(-1)].set(log_total.reshape(-1), mode="drop")
    return sums, evidence
```

```python
import jax
import jax.numpy as jnp
from jax import lax
from jax.sharding import PartitionSpec as P

AXES = ("cls", "dom")
CORE = 1


def plan(mesh):
    owners, dom = mesh.shape["cls"], mesh.shape["dom"]
    plane_bits = (dom // 2).bit_length() - 1
    masks = [2 << bit for bit in range(plane_bits)]
    if plane_bits % 2:
        return owners, dom, (masks, masks), False
    low, high = masks[: plane_bits // 2], masks[plane_bits // 2 :]
    return owners, dom, (low + high, high + low), True


def solution(mesh):
    owners, dom, orders, crossed = plan(mesh)
    devices = owners * dom
    steps = len(orders[0])

    def swap(value, masks):
        pairs = [(i, i ^ masks[i % 2]) for i in range(devices)]
        return lax.ppermute(value, AXES, pairs)

    def swap_core(value):
        return swap(value, (CORE, CORE))

    def swap_plane(value, step):
        return swap(value, (orders[0][step], orders[1][step]))

    def swap_cls(value, k):
        return swap(value, (k * dom, k * dom))

    def on_device(particles, assign, inv_sigma, projections):
        local, width = particles.shape
        half = width // 2
        per_owner, own = projections.shape[:2]
        mine_rows = per_owner * own
        first = lax.axis_index("dom") % 2 == 0

        def halves_of(value):
            low, high = value[:, :half], value[:, half:]
            return jnp.where(first, low, high), jnp.where(first, high, low)

        flat = projections.reshape(mine_rows, width)
        kept, sent = halves_of(flat)
        got = swap_core(sent)
        block = jnp.concatenate(
            [jnp.where(first, kept, got), jnp.where(first, got, kept)], axis=0
        )
        pieces = {k: swap_cls(block, k) for k in range(owners - 1, 0, -1)}
        gathered = jnp.concatenate([block] + [pieces[k] for k in range(1, owners)], axis=0)

        side = jnp.stack([inv_sigma.astype(jnp.float32), assign[:, 0].astype(jnp.float32)])
        side = jnp.concatenate([side, swap_core(side)], axis=1)
        precision, class_id = side[0], side[1].astype(jnp.int32)
        kept, sent = halves_of(particles)
        images = jnp.concatenate([kept, swap_core(sent)], axis=0)

        def score(rows):
            products = lax.dot_general(
                rows, images, (((1,), (1,)), ((), ())), preferred_element_type=jnp.float32
            )
            norms = 0.5 * jnp.sum(jnp.square(rows.astype(jnp.float32)), axis=1)
            return products - norms[:, None]

        partial = [score(gathered)]
        for step in range(steps):
            fresh = swap_plane(gathered, step)
            partial.append(score(fresh))
            gathered = jnp.concatenate([gathered, fresh], axis=0)
        partial = jnp.concatenate(partial, axis=0)
        rows = partial.shape[0]
        other = swap_core(partial)
        if crossed:
            side_len = 1 << (steps // 2)
            other = other.reshape(side_len, side_len, -1, 2 * local).transpose(1, 0, 2, 3)
        other = other.reshape(rows, 2, local)[:, ::-1].reshape(rows, 2 * local)
        scores = precision[None, :] * (partial + other)

        z = lax.axis_index("cls") ^ jnp.arange(owners, dtype=jnp.int32)
        kind = z[:, None] * per_owner + jnp.arange(per_owner, dtype=jnp.int32)[None, :]
        kind = jnp.broadcast_to(
            kind[None, :, None, :, None], (rows // (2 * mine_rows * owners), owners, 2, per_owner, own)
        ).reshape(rows)
        named = kind[:, None] == class_id[None, :]
        largest = jnp.max(jnp.where(named, scores, -jnp.inf), axis=0)
        exponent = jnp.where(named, jnp.exp(jnp.where(named, scores - largest[None, :], 0.0)), 0.0)
        totals = jnp.sum(exponent, axis=0)
        weights = (exponent / totals[None, :]).astype(jnp.bfloat16)
        evidence = (largest + jnp.log(totals))[:local]

        def weigh(part, kind):
            return jnp.dot(part, images, preferred_element_type=jnp.float32).astype(kind)

        middle = rows // 2
        fresh = swap_plane(weigh(weights[middle:], jnp.bfloat16), steps - 1)
        sums = weigh(weights[:middle], jnp.float32) + fresh.astype(jnp.float32)
        for step in range(steps - 2, -1, -1):
            middle = sums.shape[0] // 2
            sums = sums[:middle] + swap_plane(sums[middle:], step)
        size = 2 * mine_rows
        total = sums[:size]
        for k in range(owners - 1, 0, -1):
            part = sums[k * size : (k + 1) * size]
            if k > 1:
                part = part.astype(jnp.bfloat16)
            total = total + swap_cls(part, k).astype(jnp.float32)
        low, high = total[:mine_rows], total[mine_rows:]
        kept, sent = jnp.where(first, low, high), jnp.where(first, high, low)
        got = swap_core(sent)
        class_sums = jnp.concatenate(
            [jnp.where(first, kept, got), jnp.where(first, got, kept)], axis=1
        )
        return class_sums.reshape(per_owner, own, width), evidence

    return jax.shard_map(
        on_device,
        mesh=mesh,
        in_specs=(
            P(("cls", "dom"), None),
            P(("cls", "dom"), None),
            P(("cls", "dom")),
            P("cls", "dom", None),
        ),
        out_specs=(P("cls", "dom", None), P(("cls", "dom"))),
        check_vma=False,
    )
```

```python
import jax
import jax.numpy as jnp
from jax import lax
from jax.sharding import PartitionSpec as P

AXES = ("cls", "dom")
CORE = 1


def plan(mesh):
    owners, dom = mesh.shape["cls"], mesh.shape["dom"]
    plane_bits = (dom // 2).bit_length() - 1
    masks = [2 << bit for bit in range(plane_bits)]
    if plane_bits % 2:
        return owners, dom, (masks, masks), False
    low, high = masks[: plane_bits // 2], masks[plane_bits // 2 :]
    return owners, dom, (low + high, high + low), True


def solution(mesh):
    owners, dom, orders, crossed = plan(mesh)
    devices = owners * dom
    steps = len(orders[0])

    def swap(value, masks):
        pairs = [(i, i ^ masks[i % 2]) for i in range(devices)]
        return lax.ppermute(value, AXES, pairs)

    def swap_core(value):
        return swap(value, (CORE, CORE))

    def swap_plane(value, step):
        return swap(value, (orders[0][step], orders[1][step]))

    def swap_cls(value, k):
        return swap(value, (k * dom, k * dom))

    def on_device(particles, assign, inv_sigma, projections):
        local, width = particles.shape
        half = width // 2
        per_owner, own = projections.shape[:2]
        mine_rows = per_owner * own
        first = lax.axis_index("dom") % 2 == 0

        def halves_of(value):
            low, high = value[:, :half], value[:, half:]
            return jnp.where(first, low, high), jnp.where(first, high, low)

        flat = projections.reshape(mine_rows, width)
        kept, sent = halves_of(flat)
        got = swap_core(sent)
        block = jnp.concatenate(
            [jnp.where(first, kept, got), jnp.where(first, got, kept)], axis=0
        )
        near = max(owners // 2, 1)
        pieces = {k: swap_cls(block, k) for k in range(1, owners)}
        pieces[0] = block
        groups = [range(0, near)] + ([range(near, owners)] if owners > 1 else [])

        def spread(held):
            older, newer = [held], []
            for step in range(steps):
                sets = [part for part in (older, newer) if part]
                got = [swap_plane(jnp.concatenate(part, axis=0), step) for part in sets]
                older, newer = older + newer, got
            return jnp.concatenate(older + newer, axis=0)

        gathered = [spread(jnp.concatenate([pieces[k] for k in g], axis=0)) for g in groups]

        side = jnp.stack([inv_sigma.astype(jnp.float32), assign[:, 0].astype(jnp.float32)])
        side = jnp.concatenate([side, swap_core(side)], axis=1)
        precision, class_id = side[0], side[1].astype(jnp.int32)
        kept, sent = halves_of(particles)
        images = jnp.concatenate([kept, swap_core(sent)], axis=0)

        def score(rows):
            products = lax.dot_general(
                rows, images, (((1,), (1,)), ((), ())), preferred_element_type=jnp.float32
            )
            norms = 0.5 * jnp.sum(jnp.square(rows.astype(jnp.float32)), axis=1)
            return products - norms[:, None]

        partial = jnp.concatenate([score(part) for part in gathered], axis=0)
        rows = partial.shape[0]
        other = swap_core(partial)
        if crossed:
            side_len = 1 << (steps // 2)
            other = other.reshape(len(groups), side_len, side_len, -1, 2 * local)
            other = other.transpose(0, 2, 1, 3, 4)
        other = other.reshape(rows, 2, local)[:, ::-1].reshape(rows, 2 * local)
        scores = precision[None, :] * (partial + other)

        z = lax.axis_index("cls") ^ jnp.arange(owners, dtype=jnp.int32)
        kind = z[:, None] * per_owner + jnp.arange(per_owner, dtype=jnp.int32)[None, :]
        kind = jnp.broadcast_to(
            kind.reshape(len(groups), 1, -1, 1, per_owner, 1),
            (len(groups), 1 << steps, owners // len(groups), 2, per_owner, own),
        ).reshape(rows)
        named = kind[:, None] == class_id[None, :]
        largest = jnp.max(jnp.where(named, scores, -jnp.inf), axis=0)
        exponent = jnp.where(named, jnp.exp(jnp.where(named, scores - largest[None, :], 0.0)), 0.0)
        totals = jnp.sum(exponent, axis=0)
        weights = (exponent / totals[None, :]).astype(jnp.bfloat16)
        evidence = (largest + jnp.log(totals))[:local]

        def weigh(part):
            return jnp.dot(part, images, preferred_element_type=jnp.float32)

        size = 2 * mine_rows

        def reduce(part):
            for step in range(steps - 1, -1, -1):
                kind = jnp.bfloat16 if step == steps - 1 else jnp.float32
                count = part.shape[0] // 2
                keep, send = part[:count], part[count:].astype(kind)
                if step:
                    far = swap_plane(send[count // 2 :], step).astype(jnp.float32)
                    close = swap_plane(send[: count // 2], step).astype(jnp.float32)
                    part = jnp.concatenate(
                        [keep[: count // 2] + close, keep[count // 2 :] + far], axis=0
                    )
                else:
                    part = keep + swap_plane(send, step).astype(jnp.float32)
            return part

        total = None
        count = rows // len(groups)
        for i in range(len(groups) - 1, -1, -1):
            sums = reduce(weigh(weights[i * count : (i + 1) * count]))
            for j, k in enumerate(groups[i]):
                part = sums[j * size : (j + 1) * size]
                if k > 1:
                    part = part.astype(jnp.bfloat16)
                if k > 0:
                    part = swap_cls(part, k).astype(jnp.float32)
                total = part if total is None else total + part
        low, high = total[:mine_rows], total[mine_rows:]
        kept, sent = jnp.where(first, low, high), jnp.where(first, high, low)
        got = swap_core(sent)
        class_sums = jnp.concatenate(
            [jnp.where(first, kept, got), jnp.where(first, got, kept)], axis=1
        )
        return class_sums.reshape(per_owner, own, width), evidence

    return jax.shard_map(
        on_device,
        mesh=mesh,
        in_specs=(
            P(("cls", "dom"), None),
            P(("cls", "dom"), None),
            P(("cls", "dom")),
            P("cls", "dom", None),
        ),
        out_specs=(P("cls", "dom", None), P(("cls", "dom"))),
        check_vma=False,
    )
```

```python
import functools
import math

import jax
import jax.numpy as jnp
from jax import lax
from jax.experimental import pallas as pl
from jax.experimental.pallas import tpu as pltpu
from jax.sharding import PartitionSpec as P

AXES = ("cls", "dom")
CORE = 1
FLOAT, SHORT = jnp.float32, jnp.bfloat16
NT = (((1,), (1,)), ((), ()))
COSTS = {"score": [(1 << 28, 1 << 21)] * 2, "softmax": (1 << 28, 1 << 22), "weigh": (1 << 28, 1 << 22), "near": (1 << 20, 1 << 16), "sum": (1 << 31, 1 << 16)}


def plan(mesh):
    owners, dom = mesh.shape["cls"], mesh.shape["dom"]
    plane_bits = (dom // 2).bit_length() - 1
    masks = [2 << bit for bit in range(plane_bits)]
    if plane_bits % 2:
        return owners, dom, (masks, masks), False
    low, high = masks[: plane_bits // 2], masks[plane_bits // 2 :]
    return owners, dom, (low + high, high + low), True


def call(body, outs, cost, *args, smem=()):
    spaces = [
        pl.BlockSpec(memory_space=pltpu.SMEM if i in smem else pltpu.VMEM) for i in range(len(args))
    ]
    out_shape = [jax.ShapeDtypeStruct(shape, kind) for shape, kind in outs]
    held = sum(math.prod(array.shape) * array.dtype.itemsize for array in [*args, *out_shape])
    return pl.pallas_call(
        body,
        out_shape=out_shape,
        in_specs=spaces,
        out_specs=[pl.BlockSpec(memory_space=pltpu.VMEM)] * len(outs),
        compiler_params=pltpu.CompilerParams(vmem_limit_bytes=min(held + (8 << 20), 56 << 20)),
        cost_estimate=pl.CostEstimate(flops=cost[0], bytes_accessed=cost[1], transcendentals=0),
    )(*args)


def by_core(core, body):
    @pl.when(core[0] == 0)
    def _():
        body(0)

    @pl.when(core[0] != 0)
    def _():
        body(1)


def copy_body(source, out):
    out[...] = source[...]


def block_body(core, mine, theirs, out):
    quarter = out.shape[2]

    def fill(c):
        pair = (theirs, mine) if c else (mine, theirs)
        for ch in range(2):
            lo = (2 * c + ch) * quarter
            rows = [
                ref[k, :, lo : lo + quarter].astype(FLOAT) for ref in pair for k in range(ref.shape[0])
            ]
            rows = jnp.concatenate(rows, axis=0)
            out[0, ch * rows.shape[0] : (ch + 1) * rows.shape[0]] = rows.astype(SHORT)

    by_core(core, fill)


def sum_body(*refs):
    *parts, out = refs
    total = parts[0][...].astype(FLOAT)
    for part in parts[1:]:
        total += part[...].astype(FLOAT)
    out[...] = total


def near_body(*refs):
    count = sum(1 for ref in refs if ref.shape != refs[0].shape)
    parts, outs = refs[:-count], refs[-count:]
    at = 0
    for out in outs:
        total = 0.0
        for part in parts:
            total += part[at : at + out.shape[0]].astype(FLOAT)
        out[...] = total
        at += out.shape[0]


def total_body(core, *refs):
    *parts, kept, sent = refs
    rows = kept.shape[1]
    total = parts[0][0].astype(FLOAT)
    for part in parts[1:]:
        total += part[0].astype(FLOAT)

    def fill(c):
        for ch in range(2):
            at = 2 * ch * rows
            kept[ch] = total[at + c * rows : at + (c + 1) * rows]
            sent[ch] = total[at + (1 - c) * rows : at + (2 - c) * rows]

    by_core(core, fill)


def final_body(core, kept, got, out):
    quarter, (classes, own) = kept.shape[2], out.shape[:2]

    def fill(c):
        for j, part in ((c, kept), (1 - c, got)):
            for ch in range(2):
                lo = (2 * j + ch) * quarter
                for k in range(classes):
                    out[k, :, lo : lo + quarter] = part[ch, k * own : (k + 1) * own]

    by_core(core, fill)


def score_body(count, *refs):
    core, images, other, out = refs[count:]
    quarter = refs[0].shape[2]
    rows = jnp.concatenate([ref[...].reshape(-1, quarter) for ref in refs[:count]], axis=0)
    blocks = rows.shape[0] // 16
    wide = rows.astype(FLOAT)
    norms = jnp.sum(wide * wide, axis=1, keepdims=True).reshape(blocks, 16, 1)
    norms = 0.5 * (norms[:, :8] + norms[:, 8:]).reshape(blocks * 8, 1)
    local = images.shape[0]

    def fill(c):
        for j, (part, at) in enumerate(((images, 2 * c * quarter), (other, 0))):
            sums = 0.0
            for ch in range(2):
                chunk = part[:, at + ch * quarter : at + (ch + 1) * quarter]
                scores = lax.dot_general(rows, chunk, NT, preferred_element_type=FLOAT)
                sums += scores.reshape(blocks, 16, local)[:, ch * 8 : ch * 8 + 8]
            out[:, j * local : (j + 1) * local] = sums.reshape(blocks * 8, local) - norms

    by_core(core, fill)


def score(pieces, core, images, other, cost):
    blocks = sum(piece.shape[0] for piece in pieces)
    return call(
        functools.partial(score_body, len(pieces)),
        [((blocks * 8, 2 * images.shape[0]), FLOAT)],
        cost,
        *pieces,
        core,
        images,
        other,
        smem=(len(pieces),),
    )[0]


def weigh_rows(weights, core, images, other, outs):
    quarter = outs[0].shape[2]
    blocks = weights.shape[0] // 8
    step = 512
    offset = pl.multiple_of(core[0] * (2 * quarter), 128)
    for begin in range(0, quarter, step):
        halves = []
        for lo in (begin, quarter + begin):
            chunk = jnp.concatenate(
                [images[:, pl.ds(offset + lo, step)], other[:, lo : lo + step]], axis=0
            )
            sums = jnp.dot(weights, chunk, preferred_element_type=FLOAT)
            halves.append(sums.reshape(blocks, 8, step))
        at = 0
        for out in outs:
            count = out.shape[0]
            both = [sums[at : at + count] for sums in halves]
            out[:, :, begin : begin + step] = jnp.concatenate(both, axis=1).astype(out.dtype)
            at += count


def weigh_body(weights, core, images, other, *outs):
    weigh_rows(weights[...], core, images, other, outs)


def softmax_body(order, leave, cut, count, *refs):
    mine, theirs = (
        jnp.concatenate([ref[...] for ref in part], axis=0)
        for part in (refs[:count], refs[count : 2 * count])
    )
    precision, named_class, kind, core, images, other = refs[2 * count : 2 * count + 6]
    weights_near, evidence, *outs = refs[2 * count + 6 :]
    local = images.shape[0]
    theirs = jnp.concatenate([theirs[lo:hi] for lo, hi in order], axis=0)
    theirs = jnp.concatenate([theirs[:, local:], theirs[:, :local]], axis=1)
    scores = precision[...] * (mine + theirs)
    named = kind[...] == named_class[...]
    largest = jnp.max(jnp.where(named, scores, -jnp.inf), axis=0, keepdims=True)
    exponent = jnp.where(named, jnp.exp(jnp.where(named, scores - largest, 0.0)), 0.0)
    totals = jnp.sum(exponent, axis=0, keepdims=True)
    weights = exponent / totals
    weights = jnp.concatenate([weights[lo:hi] for lo, hi in leave], axis=0).astype(SHORT)
    evidence[...] = largest + jnp.log(totals)
    weights_near[...] = weights[:cut]
    weigh_rows(weights[cut:], core, images, other, outs)


def part_body(core, images, sent):
    half = sent.shape[1]

    def fill(c):
        sent[...] = images[:, (1 - c) * half : (2 - c) * half]

    by_core(core, fill)


def solution(mesh):
    owners, dom, orders, crossed = plan(mesh)
    devices = owners * dom
    steps = len(orders[0])
    near_count = max(owners // 2, 1)
    groups = [range(0, near_count)] + ([range(near_count, owners)] if owners > 1 else [])

    def swap(value, masks, name):
        pairs = [(i, i ^ masks[i % 2]) for i in range(devices)]
        with jax.named_scope(name):
            return lax.ppermute(value, AXES, pairs)

    def swap_core(value, name):
        return swap(value, (CORE, CORE), "core_" + name)

    def swap_plane(value, step, name):
        return swap(value, (orders[0][step], orders[1][step]), f"plane{step}_{name}")

    def swap_cls(value, k, name):
        return swap(value, (k * dom, k * dom), f"cls{k}_{name}")

    def on_device(particles, assign, inv_sigma, projections):
        local, width = particles.shape
        half, quarter = width // 2, width // 4
        per_owner, own = projections.shape[:2]
        mine_rows = per_owner * own
        size = 2 * mine_rows
        core = lax.axis_index("dom") % 2
        where = core.astype(jnp.int32)[None]

        got = swap_core(projections, "rows")
        rows = call(
            copy_body, [(projections.shape, SHORT)], (0, 4 * mine_rows * width), projections
        )[0]
        block = call(
            block_body,
            [((1, 2 * size, quarter), SHORT)],
            (0, 3 * size * half),
            where,
            rows,
            got,
            smem=(0,),
        )[0]
        pieces = {k: swap_cls(block, k, "rows") for k in range(1, owners)}
        pieces[0] = block

        def spread(held, name):
            older, newer = [held], []
            for step in range(steps):
                sets = [part for part in (older, newer) if part]
                got = [
                    swap_plane(jnp.concatenate(part, axis=0), step, f"{name}{i}")
                    for i, part in enumerate(sets)
                ]
                older, newer = older + newer, got
            return older + newer

        gathered = [
            spread(jnp.concatenate([pieces[k] for k in g], axis=0), f"rows{i}")
            for i, g in enumerate(groups)
        ]

        late, late_assign, late_sigma, _ = lax.optimization_barrier(
            (particles, assign, inv_sigma, got)
        )
        side = jnp.stack([late_sigma.astype(FLOAT), late_assign[:, 0].astype(FLOAT)])
        side = jnp.concatenate([side, swap_core(side, "side")], axis=1)
        precision, class_id = side[:1], side[1:].astype(jnp.int32)
        sent = call(
            part_body, [((local, half), SHORT)], (0, 4 * local * half), where, late, smem=(0,)
        )[0]
        other = swap_core(sent, "images")

        partial = [score(gathered[0], where, particles, other, COSTS["score"][0])]
        others = [swap_core(partial[0], "scores0")]
        if len(gathered) > 1:
            gathered[1][-1], others[0] = lax.optimization_barrier((gathered[1][-1], others[0]))
            partial.append(score(gathered[1], where, particles, other, COSTS["score"][1]))
            others.append(swap_core(partial[1], "scores1"))
        rows_far = partial[0].shape[0]
        rows = rows_far * len(groups)

        positions = 1 << steps
        each = rows_far // positions
        side_len = 1 << (steps // 2)
        order = []
        for g in range(len(groups)):
            for p in range(positions):
                q = p % side_len * side_len + p // side_len if crossed else p
                begin = g * rows_far + q * each
                order.append((begin, begin + each))

        z = lax.axis_index("cls") ^ jnp.arange(owners, dtype=jnp.int32)
        kind = z[:, None] * per_owner + jnp.arange(per_owner, dtype=jnp.int32)[None, :]
        kind = jnp.broadcast_to(
            kind.reshape(len(groups), 1, -1, 1, per_owner, 1),
            (len(groups), positions, owners // len(groups), 2, per_owner, own),
        ).reshape(rows, 1)

        stays, goes = [], []
        unit = each // near_count
        for p in range(positions):
            stays.append((p * each, p * each + unit))
        for j in range(1, near_count):
            goes += [(p * each + j * unit, p * each + (j + 1) * unit) for p in range(positions)]
        specs_stay = [((positions, 2 * size, quarter), FLOAT)]
        specs_go = [((positions, 2 * size, quarter), SHORT)] * (near_count - 1)
        keeps = 2 if steps > 1 else 1
        if owners > 1:
            stays.append((rows_far, rows_far + rows_far // 2))
            goes.append((rows_far + rows_far // 2, rows))
            count = rows_far // size // (2 * keeps)
            specs_stay += [((count, 2 * size, quarter), FLOAT)] * keeps
            specs_go += [((count, 2 * size, quarter), SHORT)] * keeps
        cut = sum(hi - lo for lo, hi in stays)
        weights, evidence, *sends = call(
            functools.partial(softmax_body, order, stays + goes, cut, len(partial)),
            [((cut, 2 * local), SHORT), ((1, 2 * local), FLOAT)] + specs_go,
            COSTS["softmax"],
            *partial,
            *others,
            precision,
            class_id,
            kind,
            where,
            particles,
            other,
            smem=(2 * len(partial) + 3,),
        )
        held, *kept = call(
            weigh_body, specs_stay, COSTS["weigh"], weights, where, particles, other, smem=(1,)
        )

        ends = []
        if owners > 1:
            far = sends[near_count - 1 :]
            fresh = [swap_plane(far[i], steps - 1, f"far{i}") for i in range(keeps)[::-1]][::-1]
            kept = [part + new.astype(FLOAT) for part, new in zip(kept, fresh, strict=True)]
            for step in range(steps - 2, -1, -1):
                stay, send = kept
                if step == steps - 2:
                    send = send.astype(SHORT)
                if step == 0:
                    kept = [stay + swap_plane(send, step, "far").astype(FLOAT)]
                    continue
                n = stay.shape[0] // 2
                away = stay[n:] + swap_plane(send[n:], step, "far1").astype(FLOAT)
                kept = [stay[:n] + swap_plane(send[:n], step, "far0").astype(FLOAT), away]
            for j, k in enumerate(groups[1]):
                ends.append(swap_cls(kept[0][j : j + 1].astype(SHORT), k, "far"))
            ends = call(sum_body, [((1, 2 * size, quarter), FLOAT)], COSTS["sum"], *ends)
        near = [swap_cls(part, k, "near") for k, part in enumerate(sends[: near_count - 1], 1)]
        pieces = [((1, 2 * size, quarter), FLOAT)] * positions
        held = call(near_body, pieces, COSTS["near"], held, *near)
        ends = [held[0], *ends]
        for q in range(positions - 1, 0, -1):
            masks = [
                functools.reduce(int.__xor__, [m for s, m in enumerate(way) if q >> s & 1])
                for way in orders
            ]
            ends.append(swap(held[q], masks, f"plane_own{q}"))
        kept, sent = call(
            total_body,
            [((2, mine_rows, quarter), FLOAT)] * 2,
            (0, 8 * size * half),
            where,
            *ends,
            smem=(0,),
        )
        got = swap_core(sent, "sums")
        class_sums = call(
            final_body,
            [((per_owner, own, width), FLOAT)],
            (0, 8 * mine_rows * width),
            where,
            kept,
            got,
            smem=(0,),
        )[0]
        return class_sums, evidence[0, :local]

    return jax.shard_map(
        on_device,
        mesh=mesh,
        in_specs=(
            P(("cls", "dom"), None),
            P(("cls", "dom"), None),
            P(("cls", "dom")),
            P("cls", "dom", None),
        ),
        out_specs=(P("cls", "dom", None), P(("cls", "dom"))),
        check_vma=False,
    )
```

```python
import functools
import math

import jax
import jax.numpy as jnp
from jax import lax
from jax.experimental import pallas as pl
from jax.experimental.pallas import tpu as pltpu
from jax.sharding import PartitionSpec as P

AXES = ("cls", "dom")
CORE = 1
FLOAT, SHORT = jnp.float32, jnp.bfloat16
NT = (((1,), (1,)), ((), ()))
COSTS = {
    "part": (1 << 30, 1 << 20),
    "near_score": (1 << 28, 1 << 21),
    "far_score": (1 << 20, 1 << 20),
    "softmax": (1 << 28, 1 << 22),
    "weigh": (1 << 28, 1 << 22),
    "near": (1 << 20, 1 << 16),
    "sum": (1 << 31, 1 << 16),
}


def plan(mesh):
    owners, dom = mesh.shape["cls"], mesh.shape["dom"]
    plane_bits = (dom // 2).bit_length() - 1
    masks = [2 << bit for bit in range(plane_bits)]
    if plane_bits % 2:
        return owners, dom, (masks, masks), False
    low, high = masks[: plane_bits // 2], masks[plane_bits // 2 :]
    return owners, dom, (low + high, high + low), True


def call(body, outs, cost, *args, smem=()):
    spaces = [
        pl.BlockSpec(memory_space=pltpu.SMEM if i in smem else pltpu.VMEM) for i in range(len(args))
    ]
    out_shape = [jax.ShapeDtypeStruct(shape, kind) for shape, kind in outs]
    held = sum(math.prod(array.shape) * array.dtype.itemsize for array in [*args, *out_shape])
    return pl.pallas_call(
        body,
        out_shape=out_shape,
        in_specs=spaces,
        out_specs=[pl.BlockSpec(memory_space=pltpu.VMEM)] * len(outs),
        compiler_params=pltpu.CompilerParams(vmem_limit_bytes=min(held + (8 << 20), 56 << 20)),
        cost_estimate=pl.CostEstimate(flops=cost[0], bytes_accessed=cost[1], transcendentals=0),
    )(*args)


def by_core(core, body):
    @pl.when(core[0] == 0)
    def _():
        body(0)

    @pl.when(core[0] != 0)
    def _():
        body(1)


def copy_body(source, out):
    out[...] = source[...]


def block_body(core, mine, theirs, out):
    quarter = out.shape[2]

    def fill(c):
        pair = (theirs, mine) if c else (mine, theirs)
        for ch in range(2):
            lo = (2 * c + ch) * quarter
            rows = [
                ref[k, :, lo : lo + quarter].astype(FLOAT) for ref in pair for k in range(ref.shape[0])
            ]
            rows = jnp.concatenate(rows, axis=0)
            out[0, ch * rows.shape[0] : (ch + 1) * rows.shape[0]] = rows.astype(SHORT)

    by_core(core, fill)


def total_body(core, *refs):
    *parts, kept, sent = refs
    rows = kept.shape[1]
    total = parts[0][0].astype(FLOAT)
    for part in parts[1:]:
        total += part[0].astype(FLOAT)

    def fill(c):
        for ch in range(2):
            at = 2 * ch * rows
            kept[ch] = total[at + c * rows : at + (c + 1) * rows]
            sent[ch] = total[at + (1 - c) * rows : at + (2 - c) * rows]

    by_core(core, fill)


def final_body(core, kept, got, out):
    quarter, (classes, own) = kept.shape[2], out.shape[:2]

    def fill(c):
        for j, part in ((c, kept), (1 - c, got)):
            for ch in range(2):
                lo = (2 * j + ch) * quarter
                for k in range(classes):
                    out[k, :, lo : lo + quarter] = part[ch, k * own : (k + 1) * own]

    by_core(core, fill)


def sum_body(*refs):
    *parts, out = refs
    total = parts[0][...].astype(FLOAT)
    for part in parts[1:]:
        total += part[...].astype(FLOAT)
    out[...] = total


def near_body(*refs):
    count = sum(1 for ref in refs if ref.shape[0] != refs[0].shape[0])
    parts, outs = refs[:-count], refs[-count:]
    at = 0
    for out in outs:
        total = 0.0
        for part in parts:
            total += part[at : at + out.shape[0]].astype(FLOAT)
        out[...] = total.astype(out.dtype)
        at += out.shape[0]


def part_body(core, images, sent):
    half = sent.shape[1]

    def fill(c):
        sent[...] = images[:, (1 - c) * half : (2 - c) * half]

    by_core(core, fill)


def columns(images, other, j, c, lo, count):
    if j:
        return other[:, lo : lo + count]
    lo += c * other.shape[1]
    return images[:, lo : lo + count]


def score_body(count, *refs):
    core, images, other, out = refs[count:]
    quarter = refs[0].shape[2]
    rows = jnp.concatenate([ref[...].reshape(-1, quarter) for ref in refs[:count]], axis=0)
    blocks = rows.shape[0] // 16
    wide = rows.astype(FLOAT)
    norms = jnp.sum(wide * wide, axis=1, keepdims=True).reshape(blocks, 16, 1)
    norms = 0.5 * (norms[:, :8] + norms[:, 8:]).reshape(blocks * 8, 1)
    local = images.shape[0]

    def fill(c):
        for j in range(2):
            sums = 0.0
            for ch in range(2):
                chunk = columns(images, other, j, c, ch * quarter, quarter)
                scores = lax.dot_general(rows, chunk, NT, preferred_element_type=FLOAT)
                sums += scores.reshape(blocks, 16, local)[:, ch * 8 : ch * 8 + 8]
            out[:, j * local : (j + 1) * local] = sums.reshape(blocks * 8, local) - norms

    by_core(core, fill)


def score(pieces, core, images, other, cost):
    blocks = sum(piece.shape[0] for piece in pieces)
    return call(
        functools.partial(score_body, len(pieces)),
        [((blocks * 8, 2 * images.shape[0]), FLOAT)],
        cost,
        *pieces,
        core,
        images,
        other,
        smem=(len(pieces),),
    )[0]


def weigh_rows(weights, core, images, other, outs):
    quarter = outs[0].shape[2]
    blocks = weights.shape[0] // 8
    step = 512

    def fill(c):
        for begin in range(0, quarter, step):
            halves = []
            for lo in (begin, quarter + begin):
                chunk = [columns(images, other, j, c, lo, step) for j in range(2)]
                chunk = jnp.concatenate(chunk, axis=0)
                sums = jnp.dot(weights, chunk, preferred_element_type=FLOAT)
                halves.append(sums.reshape(blocks, 8, step))
            at = 0
            for out in outs:
                count = out.shape[0]
                both = [sums[at : at + count] for sums in halves]
                out[:, :, begin : begin + step] = jnp.concatenate(both, axis=1).astype(out.dtype)
                at += count

    by_core(core, fill)


def weigh_body(weights, core, images, other, *outs):
    weigh_rows(weights[...], core, images, other, outs)


def softmax_body(order, places, per_owner, own, leave, cut, count, *refs):
    mine, theirs = (
        jnp.concatenate([ref[...] for ref in part], axis=0)
        for part in (refs[:count], refs[count : 2 * count])
    )
    precision, named_class, place, core, images, other = refs[2 * count : 2 * count + 6]
    weights_near, evidence, *outs = refs[2 * count + 6 :]
    local = images.shape[0]
    theirs = jnp.concatenate([theirs[lo:hi] for lo, hi in order], axis=0)
    theirs = jnp.concatenate([theirs[:, local:], theirs[:, :local]], axis=1)
    scores = precision[...] * (mine + theirs)
    rows = lax.broadcasted_iota(jnp.int32, (2 * per_owner * own, 2 * local), 0)
    rows = lax.rem(lax.div(rows, own), per_owner)
    kind = [rows + (place[0] ^ k) * per_owner for k in places]
    named = jnp.concatenate(kind, axis=0) == named_class[...]
    largest = jnp.max(jnp.where(named, scores, -jnp.inf), axis=0, keepdims=True)
    exponent = jnp.where(named, jnp.exp(jnp.where(named, scores - largest, 0.0)), 0.0)
    totals = jnp.sum(exponent, axis=0, keepdims=True)
    weights = exponent / totals
    weights = jnp.concatenate([weights[lo:hi] for lo, hi in leave], axis=0).astype(SHORT)
    evidence[...] = largest + jnp.log(totals)
    weights_near[...] = weights[:cut]
    weigh_rows(weights[cut:], core, images, other, outs)


def solution(mesh):
    owners, dom, orders, crossed = plan(mesh)
    devices = owners * dom
    steps = len(orders[0])
    positions = 1 << steps
    near_count = max(owners // 2, 1)
    far_count = owners - near_count

    def swap(value, masks, name):
        pairs = [(i, i ^ masks[i % 2]) for i in range(devices)]
        with jax.named_scope(name):
            return lax.ppermute(value, AXES, pairs)

    def masks_of(q):
        return [
            functools.reduce(int.__xor__, [m for s, m in enumerate(way) if q >> s & 1])
            for way in orders
        ]

    def swap_core(value, name):
        return swap(value, (CORE, CORE), "core_" + name)

    def swap_plane(value, step, name):
        return swap(value, (orders[0][step], orders[1][step]), f"plane{step}_{name}")

    def swap_cls(value, k, name):
        return swap(value, (k * dom, k * dom), f"cls{k}_{name}")

    def on_device(particles, assign, inv_sigma, projections):
        local, width = particles.shape
        half, quarter = width // 2, width // 4
        per_owner, own = projections.shape[:2]
        mine_rows = per_owner * own
        size = 2 * mine_rows
        core = lax.axis_index("dom") % 2
        where = core.astype(jnp.int32)[None]
        place = lax.axis_index("cls").astype(jnp.int32)[None]
        got = swap_core(projections, "rows")
        rows = call(
            copy_body, [(projections.shape, SHORT)], (0, 4 * mine_rows * width), projections
        )[0]
        block = call(
            block_body, [((1, 2 * size, quarter), SHORT)], (0, 3 * size * half), where, rows, got,
            smem=(0,),
        )[0]

        def spread(held, name):
            older, newer = [held], []
            for step in range(steps):
                sets = [part for part in (older, newer) if part]
                fresh = [
                    swap_plane(jnp.concatenate(part, axis=0), step, f"{name}{i}")
                    for i, part in enumerate(sets)
                ]
                older, newer = older + newer, fresh
            return older + newer

        pieces = {0: block}
        for k in range(owners - 1, 0, -1):
            pieces[k] = swap_cls(block, k, "rows")
        groups = [range(near_count)] + ([range(near_count, owners)] if far_count else [])
        gathered = [
            spread(jnp.concatenate([pieces[k] for k in group], axis=0), f"rows{i}")
            for i, group in enumerate(groups)
        ]
        layout = [(k, q) for group in groups for q in range(positions) for k in group]

        late, late_assign, late_sigma, _ = lax.optimization_barrier(
            (particles, assign, inv_sigma, got)
        )
        side = jnp.stack([late_sigma.astype(FLOAT), late_assign[:, 0].astype(FLOAT)])
        side = jnp.concatenate([side, swap_core(side, "side")], axis=1)
        precision, class_id = side[:1], side[1:].astype(jnp.int32)
        sent = call(part_body, [((local, half), SHORT)], COSTS["part"], where, late, smem=(0,))[0]
        other = swap_core(sent, "images")

        partial = [score(gathered[0], where, particles, other, COSTS["near_score"])]
        others = [swap_core(partial[0], "scores0")]
        if far_count:
            gathered[1][-1], others[0] = lax.optimization_barrier((gathered[1][-1], others[0]))
            partial.append(score(gathered[1], where, particles, other, COSTS["far_score"]))
            others.append(swap_core(partial[1], "scores1"))

        index = {key: i for i, key in enumerate(layout)}
        side_len = 1 << (steps // 2)

        def span(key):
            return (index[key] * size, (index[key] + 1) * size)

        order = []
        for k, p in layout:
            q = p % side_len * side_len + p // side_len if crossed else p
            order.append(span((k, q)))
        places = [k for k, _ in layout]

        far_keys = [(k, q) for q in range(positions) for k in range(near_count, owners)]
        cut_far = len(far_keys) // 2
        stay_keys = [(0, q) for q in range(positions)] + far_keys[:cut_far]
        go_keys = [(k, q) for k in range(1, near_count) for q in range(positions)]
        go_keys += far_keys[cut_far:]
        leave = [span(key) for key in stay_keys + go_keys]
        cut = len(stay_keys) * size
        keeps = 2 if steps > 1 else 1
        specs_stay = [((positions, 2 * size, quarter), FLOAT)]
        specs_go = [((positions, 2 * size, quarter), SHORT)] * (near_count - 1)
        if far_count:
            count = len(far_keys) // (2 * keeps)
            specs_stay += [((count, 2 * size, quarter), FLOAT)] * keeps
            specs_go += [((count, 2 * size, quarter), SHORT)] * keeps
        weights, evidence, *sends = call(
            functools.partial(
                softmax_body, order, places, per_owner, own, leave, cut, len(partial)
            ),
            [((cut, 2 * local), SHORT), ((1, 2 * local), FLOAT)] + specs_go,
            COSTS["softmax"],
            *partial,
            *others,
            precision,
            class_id,
            place,
            where,
            particles,
            other,
            smem=(2 * len(partial) + 2, 2 * len(partial) + 3),
        )
        held, *kept = call(
            weigh_body, specs_stay, COSTS["weigh"], weights, where, particles, other, smem=(1,)
        )

        near = [swap_cls(part, k, "near") for k, part in enumerate(sends[: near_count - 1], 1)]
        ends = []
        if far_count:
            far = sends[near_count - 1 :]
            fresh = [swap_plane(far[i], steps - 1, f"far{i}") for i in range(keeps)[::-1]][::-1]
            kept = [part + new.astype(FLOAT) for part, new in zip(kept, fresh, strict=True)]
            for step in range(steps - 2, -1, -1):
                stay, send = kept
                if step == steps - 2:
                    send = send.astype(SHORT)
                if step == 0:
                    fresh = swap_plane(send, step, "far")
                    kept = [stay + fresh.astype(FLOAT)]
                    continue
                n = stay.shape[0] // 2
                away = stay[n:] + swap_plane(send[n:], step, "far1").astype(FLOAT)
                kept = [stay[:n] + swap_plane(send[:n], step, "far0").astype(FLOAT), away]
            for k in range(near_count, owners):
                j = k - near_count
                ends.append(swap_cls(kept[0][j : j + 1].astype(SHORT), k, "far"))
            ends = call(sum_body, [((1, 2 * size, quarter), FLOAT)], COSTS["sum"], *ends)
        kinds = [FLOAT] * (positions - 1) + [SHORT]
        own_parts = call(
            near_body,
            [((1, 2 * size, quarter), kind) for kind in kinds],
            COSTS["near"],
            held,
            *near,
        )
        ends = [own_parts[0], *ends]
        for q in range(positions - 1, 0, -1):
            ends.append(swap(own_parts[q], masks_of(q), f"plane_own{q}"))
        kept, sent = call(
            total_body,
            [((2, mine_rows, quarter), FLOAT)] * 2,
            (0, 8 * size * half),
            where,
            *ends,
            smem=(0,),
        )
        got = swap_core(sent, "sums")
        class_sums = call(
            final_body,
            [((per_owner, own, width), FLOAT)],
            (0, 8 * mine_rows * width),
            where,
            kept,
            got,
            smem=(0,),
        )[0]
        return class_sums, evidence[0, :local]

    return jax.shard_map(
        on_device,
        mesh=mesh,
        in_specs=(
            P(("cls", "dom"), None),
            P(("cls", "dom"), None),
            P(("cls", "dom")),
            P("cls", "dom", None),
        ),
        out_specs=(P("cls", "dom", None), P(("cls", "dom"))),
        check_vma=False,
    )
```

```python
import functools
import math

import jax
import jax.numpy as jnp
from jax import lax
from jax.experimental import pallas as pl
from jax.experimental.pallas import tpu as pltpu
from jax.sharding import PartitionSpec as P

AXES = ("cls", "dom")
CORE = 1
FLOAT, SHORT = jnp.float32, jnp.bfloat16
NT = (((1,), (1,)), ((), ()))
COSTS = {
    "part": (1 << 30, 1 << 20),
    "near_score": (1 << 28, 1 << 21),
    "far_score": (1 << 20, 1 << 20),
    "softmax": (1 << 28, 1 << 22),
    "weigh": (1 << 28, 1 << 22),
    "near": (1 << 20, 1 << 16),
    "sum": (1 << 31, 1 << 16),
}


def plan(mesh):
    owners, dom = mesh.shape["cls"], mesh.shape["dom"]
    plane_bits = (dom // 2).bit_length() - 1
    masks = [2 << bit for bit in range(plane_bits)]
    if plane_bits % 2:
        return owners, dom, (masks, masks), False
    low, high = masks[: plane_bits // 2], masks[plane_bits // 2 :]
    return owners, dom, (low + high, high + low), True


def call(body, outs, cost, *args, smem=()):
    spaces = [
        pl.BlockSpec(memory_space=pltpu.SMEM if i in smem else pltpu.VMEM) for i in range(len(args))
    ]
    out_shape = [jax.ShapeDtypeStruct(shape, kind) for shape, kind in outs]
    held = sum(math.prod(array.shape) * array.dtype.itemsize for array in [*args, *out_shape])
    return pl.pallas_call(
        body,
        out_shape=out_shape,
        in_specs=spaces,
        out_specs=[pl.BlockSpec(memory_space=pltpu.VMEM)] * len(outs),
        compiler_params=pltpu.CompilerParams(vmem_limit_bytes=min(held + (8 << 20), 56 << 20)),
        cost_estimate=pl.CostEstimate(flops=cost[0], bytes_accessed=cost[1], transcendentals=0),
    )(*args)


def by_core(core, body):
    @pl.when(core[0] == 0)
    def _():
        body(0)

    @pl.when(core[0] != 0)
    def _():
        body(1)


def copy_body(source, out):
    out[...] = source[...]


def block_body(core, mine, theirs, out):
    quarter = out.shape[2]

    def fill(c):
        pair = (theirs, mine) if c else (mine, theirs)
        for ch in range(2):
            lo = (2 * c + ch) * quarter
            rows = [
                ref[k, :, lo : lo + quarter].astype(FLOAT) for ref in pair for k in range(ref.shape[0])
            ]
            rows = jnp.concatenate(rows, axis=0)
            out[0, ch * rows.shape[0] : (ch + 1) * rows.shape[0]] = rows.astype(SHORT)

    by_core(core, fill)


def total_body(core, *refs):
    *parts, kept, sent = refs
    rows = kept.shape[1]
    total = parts[0][0].astype(FLOAT)
    for part in parts[1:]:
        total += part[0].astype(FLOAT)

    def fill(c):
        for ch in range(2):
            at = 2 * ch * rows
            kept[ch] = total[at + c * rows : at + (c + 1) * rows]
            sent[ch] = total[at + (1 - c) * rows : at + (2 - c) * rows]

    by_core(core, fill)


def final_body(core, kept, got, out):
    quarter, (classes, own) = kept.shape[2], out.shape[:2]

    def fill(c):
        for j, part in ((c, kept), (1 - c, got)):
            for ch in range(2):
                lo = (2 * j + ch) * quarter
                for k in range(classes):
                    out[k, :, lo : lo + quarter] = part[ch, k * own : (k + 1) * own]

    by_core(core, fill)


def sum_body(*refs):
    *parts, out = refs
    total = parts[0][...].astype(FLOAT)
    for part in parts[1:]:
        total += part[...].astype(FLOAT)
    out[...] = total


def near_body(*refs):
    count = sum(1 for ref in refs if ref.shape[0] != refs[0].shape[0])
    parts, outs = refs[:-count], refs[-count:]
    at = 0
    for out in outs:
        total = 0.0
        for part in parts:
            total += part[at : at + out.shape[0]].astype(FLOAT)
        out[...] = total.astype(out.dtype)
        at += out.shape[0]


def part_body(core, images, sent):
    half = sent.shape[1]

    def fill(c):
        sent[...] = images[:, (1 - c) * half : (2 - c) * half]

    by_core(core, fill)


def columns(images, other, j, c, lo, count):
    if j:
        return other[:, lo : lo + count]
    lo += c * other.shape[1]
    return images[:, lo : lo + count]


def score_body(count, *refs):
    core, images, other, out = refs[count:]
    quarter = refs[0].shape[2]
    rows = jnp.concatenate([ref[...].reshape(-1, quarter) for ref in refs[:count]], axis=0)
    blocks = rows.shape[0] // 16
    wide = rows.astype(FLOAT)
    norms = jnp.sum(wide * wide, axis=1, keepdims=True).reshape(blocks, 16, 1)
    norms = 0.5 * (norms[:, :8] + norms[:, 8:]).reshape(blocks * 8, 1)
    local = images.shape[0]

    def fill(c):
        for j in range(2):
            sums = 0.0
            for ch in range(2):
                chunk = columns(images, other, j, c, ch * quarter, quarter)
                scores = lax.dot_general(rows, chunk, NT, preferred_element_type=FLOAT)
                sums += scores.reshape(blocks, 16, local)[:, ch * 8 : ch * 8 + 8]
            out[:, j * local : (j + 1) * local] = sums.reshape(blocks * 8, local) - norms

    by_core(core, fill)


def score(pieces, core, images, other, cost):
    blocks = sum(piece.shape[0] for piece in pieces)
    return call(
        functools.partial(score_body, len(pieces)),
        [((blocks * 8, 2 * images.shape[0]), FLOAT)],
        cost,
        *pieces,
        core,
        images,
        other,
        smem=(len(pieces),),
    )[0]


def weigh_rows(weights, core, images, other, outs):
    quarter = outs[0].shape[2]
    blocks = weights.shape[0] // 8
    step = 512

    def fill(c):
        for begin in range(0, quarter, step):
            halves = []
            for lo in (begin, quarter + begin):
                chunk = [columns(images, other, j, c, lo, step) for j in range(2)]
                chunk = jnp.concatenate(chunk, axis=0)
                sums = jnp.dot(weights, chunk, preferred_element_type=FLOAT)
                halves.append(sums.reshape(blocks, 8, step))
            at = 0
            for out in outs:
                count = out.shape[0]
                both = [sums[at : at + count] for sums in halves]
                out[:, :, begin : begin + step] = jnp.concatenate(both, axis=1).astype(out.dtype)
                at += count

    by_core(core, fill)


def weigh_body(weights, core, images, other, *outs):
    weigh_rows(weights[...], core, images, other, outs)


def softmax_body(order, places, per_owner, own, leave, cut, count, *refs):
    mine, theirs = (
        jnp.concatenate([ref[...] for ref in part], axis=0)
        for part in (refs[:count], refs[count : 2 * count])
    )
    precision, named_class, place, core, images, other = refs[2 * count : 2 * count + 6]
    weights_near, evidence, *outs = refs[2 * count + 6 :]
    local = images.shape[0]
    theirs = jnp.concatenate([theirs[lo:hi] for lo, hi in order], axis=0)
    theirs = jnp.concatenate([theirs[:, local:], theirs[:, :local]], axis=1)
    scores = precision[...] * (mine + theirs)
    rows = lax.broadcasted_iota(jnp.int32, (2 * per_owner * own, 2 * local), 0)
    rows = lax.rem(lax.div(rows, own), per_owner)
    kind = [rows + (place[0] ^ k) * per_owner for k in places]
    named = jnp.concatenate(kind, axis=0) == named_class[...]
    largest = jnp.max(jnp.where(named, scores, -jnp.inf), axis=0, keepdims=True)
    exponent = jnp.where(named, jnp.exp(jnp.where(named, scores - largest, 0.0)), 0.0)
    totals = jnp.sum(exponent, axis=0, keepdims=True)
    weights = exponent / totals
    weights = jnp.concatenate([weights[lo:hi] for lo, hi in leave], axis=0).astype(SHORT)
    evidence[...] = (largest + jnp.log(totals))[:, :local]
    weights_near[...] = weights[:cut]
    weigh_rows(weights[cut:], core, images, other, outs)


def solution(mesh):
    owners, dom, orders, crossed = plan(mesh)
    devices = owners * dom
    steps = len(orders[0])
    positions = 1 << steps
    near_count = max(owners // 2, 1)
    far_count = owners - near_count

    def swap(value, masks, name):
        pairs = [(i, i ^ masks[i % 2]) for i in range(devices)]
        with jax.named_scope(name):
            return lax.ppermute(value, AXES, pairs)

    def masks_of(q):
        return [
            functools.reduce(int.__xor__, [m for s, m in enumerate(way) if q >> s & 1])
            for way in orders
        ]

    def swap_core(value, name):
        return swap(value, (CORE, CORE), "core_" + name)

    def swap_plane(value, step, name):
        return swap(value, (orders[0][step], orders[1][step]), f"plane{step}_{name}")

    def swap_cls(value, k, name):
        return swap(value, (k * dom, k * dom), f"cls{k}_{name}")

    def on_device(particles, assign, inv_sigma, projections):
        local, width = particles.shape
        half, quarter = width // 2, width // 4
        per_owner, own = projections.shape[:2]
        mine_rows = per_owner * own
        size = 2 * mine_rows
        core = lax.axis_index("dom") % 2
        where = core.astype(jnp.int32)[None]
        place = lax.axis_index("cls").astype(jnp.int32)[None]
        got = swap_core(projections, "rows")
        rows = call(
            copy_body, [(projections.shape, SHORT)], (0, 4 * mine_rows * width), projections
        )[0]
        block = call(
            block_body, [((1, 2 * size, quarter), SHORT)], (0, 3 * size * half), where, rows, got,
            smem=(0,),
        )[0]

        def spread(held, name):
            older, newer = [held], []
            for step in range(steps):
                sets = [part for part in (older, newer) if part]
                fresh = [
                    swap_plane(jnp.concatenate(part, axis=0), step, f"{name}{i}")
                    for i, part in enumerate(sets)
                ]
                older, newer = older + newer, fresh
            return older + newer

        pieces = {0: block}
        for k in range(owners - 1, 0, -1):
            pieces[k] = swap_cls(block, k, "rows")
        groups = [range(near_count)] + ([range(near_count, owners)] if far_count else [])
        gathered = [
            spread(jnp.concatenate([pieces[k] for k in group], axis=0), f"rows{i}")
            for i, group in enumerate(groups)
        ]
        layout = [(k, q) for group in groups for q in range(positions) for k in group]

        late, late_assign, late_sigma, _ = lax.optimization_barrier(
            (particles, assign, inv_sigma, got)
        )
        side = jnp.stack([late_sigma.astype(FLOAT), late_assign[:, 0].astype(FLOAT)])
        side = jnp.concatenate([side, swap_core(side, "side")], axis=1)
        precision, class_id = side[:1], side[1:].astype(jnp.int32)
        sent = call(part_body, [((local, half), SHORT)], COSTS["part"], where, late, smem=(0,))[0]
        other = swap_core(sent, "images")

        partial = [score(gathered[0], where, particles, other, COSTS["near_score"])]
        others = [swap_core(partial[0], "scores0")]
        if far_count:
            gathered[1][-1], others[0] = lax.optimization_barrier((gathered[1][-1], others[0]))
            partial.append(score(gathered[1], where, particles, other, COSTS["far_score"]))
            others.append(swap_core(partial[1], "scores1"))

        index = {key: i for i, key in enumerate(layout)}
        side_len = 1 << (steps // 2)

        def span(key):
            return (index[key] * size, (index[key] + 1) * size)

        order = []
        for k, p in layout:
            q = p % side_len * side_len + p // side_len if crossed else p
            order.append(span((k, q)))
        places = [k for k, _ in layout]

        far_keys = [(k, q) for q in range(positions) for k in range(near_count, owners)]
        cut_far = len(far_keys) // 2
        stay_keys = [(0, q) for q in range(positions)] + far_keys[:cut_far]
        go_keys = [(k, q) for k in range(1, near_count) for q in range(positions)]
        go_keys += far_keys[cut_far:]
        leave = [span(key) for key in stay_keys + go_keys]
        cut = len(stay_keys) * size
        keeps = 2 if steps > 1 else 1
        specs_stay = [((positions, 2 * size, quarter), FLOAT)]
        specs_go = [((positions, 2 * size, quarter), SHORT)] * (near_count - 1)
        if far_count:
            count = len(far_keys) // (2 * keeps)
            specs_stay += [((count, 2 * size, quarter), FLOAT)] * keeps
            specs_go += [((count, 2 * size, quarter), SHORT)] * keeps
        weights, evidence, *sends = call(
            functools.partial(
                softmax_body, order, places, per_owner, own, leave, cut, len(partial)
            ),
            [((cut, 2 * local), SHORT), ((1, local), FLOAT)] + specs_go,
            COSTS["softmax"],
            *partial,
            *others,
            precision,
            class_id,
            place,
            where,
            particles,
            other,
            smem=(2 * len(partial) + 2, 2 * len(partial) + 3),
        )
        held, *kept = call(
            weigh_body, specs_stay, COSTS["weigh"], weights, where, particles, other, smem=(1,)
        )

        near = [swap_cls(part, k, "near") for k, part in enumerate(sends[: near_count - 1], 1)]
        ends = []
        if far_count:
            far = sends[near_count - 1 :]
            fresh = [swap_plane(far[i], steps - 1, f"far{i}") for i in range(keeps)[::-1]][::-1]
            kept = [part + new.astype(FLOAT) for part, new in zip(kept, fresh, strict=True)]
            for step in range(steps - 2, -1, -1):
                stay, send = kept
                if step == steps - 2:
                    send = send.astype(SHORT)
                if step == 0:
                    fresh = swap_plane(send, step, "far")
                    kept = [stay + fresh.astype(FLOAT)]
                    continue
                n = stay.shape[0] // 2
                away = stay[n:] + swap_plane(send[n:], step, "far1").astype(FLOAT)
                kept = [stay[:n] + swap_plane(send[:n], step, "far0").astype(FLOAT), away]
            for k in range(near_count, owners):
                j = k - near_count
                ends.append(swap_cls(kept[0][j : j + 1].astype(SHORT), k, "far"))
            ends = call(sum_body, [((1, 2 * size, quarter), FLOAT)], COSTS["sum"], *ends)
        kinds = [FLOAT] * (positions - 1) + [SHORT]
        own_parts = call(
            near_body,
            [((1, 2 * size, quarter), kind) for kind in kinds],
            COSTS["near"],
            held,
            *near,
        )
        ends = [own_parts[0], *ends]
        for q in range(positions - 1, 0, -1):
            ends.append(swap(own_parts[q], masks_of(q), f"plane_own{q}"))
        kept, sent = call(
            total_body,
            [((2, mine_rows, quarter), FLOAT)] * 2,
            (0, 8 * size * half),
            where,
            *ends,
            smem=(0,),
        )
        got = swap_core(sent, "sums")
        class_sums = call(
            final_body,
            [((per_owner, own, width), FLOAT)],
            (0, 8 * mine_rows * width),
            where,
            kept,
            got,
            smem=(0,),
        )[0]
        return class_sums, evidence.reshape(local)

    return jax.shard_map(
        on_device,
        mesh=mesh,
        in_specs=(
            P(("cls", "dom"), None),
            P(("cls", "dom"), None),
            P(("cls", "dom")),
            P("cls", "dom", None),
        ),
        out_specs=(P("cls", "dom", None), P(("cls", "dom"))),
        check_vma=False,
    )
```

```python
import functools
import math

import jax
import jax.numpy as jnp
from jax import lax
from jax.experimental import pallas as pl
from jax.experimental.pallas import tpu as pltpu
from jax.sharding import PartitionSpec as P

AXES = ("cls", "dom")
CORE = 1
FLOAT, SHORT = jnp.float32, jnp.bfloat16
NT = (((1,), (1,)), ((), ()))
COSTS = {
    "part": (1 << 32, 1 << 20),
    "near_score": (1 << 28, 1 << 21),
    "far_score": (1 << 20, 1 << 20),
    "softmax": (1 << 28, 1 << 22),
    "weigh": (1 << 28, 1 << 22),
    "near": (1 << 20, 1 << 16),
    "sum": (1 << 31, 1 << 16),
}


def plan(mesh):
    owners, dom = mesh.shape["cls"], mesh.shape["dom"]
    plane_bits = (dom // 2).bit_length() - 1
    masks = [2 << bit for bit in range(plane_bits)]
    if plane_bits % 2:
        return owners, dom, (masks, masks), False
    low, high = masks[: plane_bits // 2], masks[plane_bits // 2 :]
    return owners, dom, (low + high, high + low), True


def call(body, outs, cost, *args, smem=()):
    spaces = [
        pl.BlockSpec(memory_space=pltpu.SMEM if i in smem else pltpu.VMEM) for i in range(len(args))
    ]
    out_shape = [jax.ShapeDtypeStruct(shape, kind) for shape, kind in outs]
    held = sum(math.prod(array.shape) * array.dtype.itemsize for array in [*args, *out_shape])
    return pl.pallas_call(
        body,
        out_shape=out_shape,
        in_specs=spaces,
        out_specs=[pl.BlockSpec(memory_space=pltpu.VMEM)] * len(outs),
        compiler_params=pltpu.CompilerParams(vmem_limit_bytes=min(held + (8 << 20), 56 << 20)),
        cost_estimate=pl.CostEstimate(flops=cost[0], bytes_accessed=cost[1], transcendentals=0),
    )(*args)


def by_core(core, body):
    @pl.when(core[0] == 0)
    def _():
        body(0)

    @pl.when(core[0] != 0)
    def _():
        body(1)


def copy_body(source, out):
    out[...] = source[...]


def block_body(core, mine, theirs, out):
    quarter = out.shape[2]

    def fill(c):
        pair = (theirs, mine) if c else (mine, theirs)
        for ch in range(2):
            lo = (2 * c + ch) * quarter
            rows = [
                ref[k, :, lo : lo + quarter].astype(FLOAT) for ref in pair for k in range(ref.shape[0])
            ]
            rows = jnp.concatenate(rows, axis=0)
            out[0, ch * rows.shape[0] : (ch + 1) * rows.shape[0]] = rows.astype(SHORT)

    by_core(core, fill)


def total_body(core, *refs):
    *parts, kept, sent = refs
    rows = kept.shape[1]
    total = parts[0][0].astype(FLOAT)
    for part in parts[1:]:
        total += part[0].astype(FLOAT)

    def fill(c):
        for ch in range(2):
            at = 2 * ch * rows
            kept[ch] = total[at + c * rows : at + (c + 1) * rows]
            sent[ch] = total[at + (1 - c) * rows : at + (2 - c) * rows]

    by_core(core, fill)


def final_body(core, kept, got, out):
    quarter, (classes, own) = kept.shape[2], out.shape[:2]

    def fill(c):
        for j, part in ((c, kept), (1 - c, got)):
            for ch in range(2):
                lo = (2 * j + ch) * quarter
                for k in range(classes):
                    out[k, :, lo : lo + quarter] = part[ch, k * own : (k + 1) * own]

    by_core(core, fill)


def sum_body(*refs):
    *parts, out = refs
    total = parts[0][...].astype(FLOAT)
    for part in parts[1:]:
        total += part[...].astype(FLOAT)
    out[...] = total


def near_body(*refs):
    count = sum(1 for ref in refs if ref.shape[0] != refs[0].shape[0])
    parts, outs = refs[:-count], refs[-count:]
    at = 0
    for out in outs:
        total = 0.0
        for part in parts:
            total += part[at : at + out.shape[0]].astype(FLOAT)
        out[...] = total.astype(out.dtype)
        at += out.shape[0]


def part_body(core, images, sent):
    half = sent.shape[1]

    def fill(c):
        sent[...] = images[:, (1 - c) * half : (2 - c) * half]

    by_core(core, fill)


def columns(images, other, j, c, lo, count):
    if j:
        return other[:, lo : lo + count]
    lo += c * other.shape[1]
    return images[:, lo : lo + count]


def score_body(count, *refs):
    core, images, other, out = refs[count:]
    quarter = refs[0].shape[2]
    rows = jnp.concatenate([ref[...].reshape(-1, quarter) for ref in refs[:count]], axis=0)
    blocks = rows.shape[0] // 16
    wide = rows.astype(FLOAT)
    norms = jnp.sum(wide * wide, axis=1, keepdims=True).reshape(blocks, 16, 1)
    norms = 0.5 * (norms[:, :8] + norms[:, 8:]).reshape(blocks * 8, 1)
    local = images.shape[0]

    def fill(c):
        for j in range(2):
            sums = 0.0
            for ch in range(2):
                chunk = columns(images, other, j, c, ch * quarter, quarter)
                scores = lax.dot_general(rows, chunk, NT, preferred_element_type=FLOAT)
                sums += scores.reshape(blocks, 16, local)[:, ch * 8 : ch * 8 + 8]
            out[:, j * local : (j + 1) * local] = sums.reshape(blocks * 8, local) - norms

    by_core(core, fill)


def score(pieces, core, images, other, cost):
    blocks = sum(piece.shape[0] for piece in pieces)
    return call(
        functools.partial(score_body, len(pieces)),
        [((blocks * 8, 2 * images.shape[0]), FLOAT)],
        cost,
        *pieces,
        core,
        images,
        other,
        smem=(len(pieces),),
    )[0]


def weigh_rows(weights, core, images, other, outs):
    quarter = outs[0].shape[2]
    blocks = weights.shape[0] // 8
    step = 512

    def fill(c):
        for begin in range(0, quarter, step):
            halves = []
            for lo in (begin, quarter + begin):
                chunk = [columns(images, other, j, c, lo, step) for j in range(2)]
                chunk = jnp.concatenate(chunk, axis=0)
                sums = jnp.dot(weights, chunk, preferred_element_type=FLOAT)
                halves.append(sums.reshape(blocks, 8, step))
            at = 0
            for out in outs:
                count = out.shape[0]
                both = [sums[at : at + count] for sums in halves]
                out[:, :, begin : begin + step] = jnp.concatenate(both, axis=1).astype(out.dtype)
                at += count

    by_core(core, fill)


def weigh_body(weights, core, images, other, *outs):
    weigh_rows(weights[...], core, images, other, outs)


def softmax_body(order, places, per_owner, own, leave, cut, count, *refs):
    mine, theirs = (
        jnp.concatenate([ref[...] for ref in part], axis=0)
        for part in (refs[:count], refs[count : 2 * count])
    )
    precision, named_class, place, core, images, other = refs[2 * count : 2 * count + 6]
    weights_near, evidence, *outs = refs[2 * count + 6 :]
    local = images.shape[0]
    theirs = jnp.concatenate([theirs[lo:hi] for lo, hi in order], axis=0)
    theirs = jnp.concatenate([theirs[:, local:], theirs[:, :local]], axis=1)
    scores = precision[...] * (mine + theirs)
    rows = lax.broadcasted_iota(jnp.int32, (2 * per_owner * own, 2 * local), 0)
    rows = lax.rem(lax.div(rows, own), per_owner)
    kind = [rows + (place[0] ^ k) * per_owner for k in places]
    named = jnp.concatenate(kind, axis=0) == named_class[...]
    largest = jnp.max(jnp.where(named, scores, -jnp.inf), axis=0, keepdims=True)
    exponent = jnp.where(named, jnp.exp(jnp.where(named, scores - largest, 0.0)), 0.0)
    totals = jnp.sum(exponent, axis=0, keepdims=True)
    weights = exponent / totals
    weights = jnp.concatenate([weights[lo:hi] for lo, hi in leave], axis=0).astype(SHORT)
    evidence[...] = largest + jnp.log(totals)
    weights_near[...] = weights[:cut]
    weigh_rows(weights[cut:], core, images, other, outs)


def solution(mesh):
    owners, dom, orders, crossed = plan(mesh)
    devices = owners * dom
    steps = len(orders[0])
    positions = 1 << steps
    near_count = max(owners // 2, 1)
    far_count = owners - near_count

    def swap(value, masks, name):
        pairs = [(i, i ^ masks[i % 2]) for i in range(devices)]
        with jax.named_scope(name):
            return lax.ppermute(value, AXES, pairs)

    def masks_of(q):
        return [
            functools.reduce(int.__xor__, [m for s, m in enumerate(way) if q >> s & 1])
            for way in orders
        ]

    def swap_core(value, name):
        return swap(value, (CORE, CORE), "core_" + name)

    def swap_plane(value, step, name):
        return swap(value, (orders[0][step], orders[1][step]), f"plane{step}_{name}")

    def swap_cls(value, k, name):
        return swap(value, (k * dom, k * dom), f"cls{k}_{name}")

    def on_device(particles, assign, inv_sigma, projections):
        local, width = particles.shape
        half, quarter = width // 2, width // 4
        per_owner, own = projections.shape[:2]
        mine_rows = per_owner * own
        size = 2 * mine_rows
        core = lax.axis_index("dom") % 2
        where = core.astype(jnp.int32)[None]
        place = lax.axis_index("cls").astype(jnp.int32)[None]
        got = swap_core(projections, "rows")
        rows = call(
            copy_body, [(projections.shape, SHORT)], (0, 4 * mine_rows * width), projections
        )[0]
        block = call(
            block_body, [((1, 2 * size, quarter), SHORT)], (0, 3 * size * half), where, rows, got,
            smem=(0,),
        )[0]

        def spread(held, name):
            older, newer = [held], []
            for step in range(steps):
                sets = [part for part in (older, newer) if part]
                fresh = [
                    swap_plane(jnp.concatenate(part, axis=0), step, f"{name}{i}")
                    for i, part in enumerate(sets)
                ]
                older, newer = older + newer, fresh
            return older + newer

        pieces = {0: block}
        for k in range(owners - 1, 0, -1):
            pieces[k] = swap_cls(block, k, "rows")
        groups = [range(near_count)] + ([range(near_count, owners)] if far_count else [])
        gathered = [
            spread(jnp.concatenate([pieces[k] for k in group], axis=0), f"rows{i}")
            for i, group in enumerate(groups)
        ]
        layout = [(k, q) for group in groups for q in range(positions) for k in group]

        late, late_assign, late_sigma, _ = lax.optimization_barrier(
            (particles, assign, inv_sigma, got)
        )
        side = jnp.stack([late_sigma.astype(FLOAT), late_assign[:, 0].astype(FLOAT)])
        side = jnp.concatenate([side, swap_core(side, "side")], axis=1)
        precision, class_id = side[:1], side[1:].astype(jnp.int32)
        sent = call(part_body, [((local, half), SHORT)], COSTS["part"], where, late, smem=(0,))[0]
        other = swap_core(sent, "images")

        partial = [score(gathered[0], where, particles, other, COSTS["near_score"])]
        others = [swap_core(partial[0], "scores0")]
        if far_count:
            gathered[1][-1], others[0] = lax.optimization_barrier((gathered[1][-1], others[0]))
            partial.append(score(gathered[1], where, particles, other, COSTS["far_score"]))
            others.append(swap_core(partial[1], "scores1"))

        index = {key: i for i, key in enumerate(layout)}
        side_len = 1 << (steps // 2)

        def span(key):
            return (index[key] * size, (index[key] + 1) * size)

        order = []
        for k, p in layout:
            q = p % side_len * side_len + p // side_len if crossed else p
            order.append(span((k, q)))
        places = [k for k, _ in layout]

        far_keys = [(k, q) for q in range(positions) for k in range(near_count, owners)]
        cut_far = len(far_keys) // 2
        stay_keys = [(0, q) for q in range(positions)] + far_keys[:cut_far]
        go_keys = [(k, q) for k in range(1, near_count) for q in range(positions)]
        go_keys += far_keys[cut_far:]
        leave = [span(key) for key in stay_keys + go_keys]
        cut = len(stay_keys) * size
        keeps = 2 if steps > 1 else 1
        specs_stay = [((positions, 2 * size, quarter), FLOAT)]
        specs_go = [((positions, 2 * size, quarter), SHORT)] * (near_count - 1)
        if far_count:
            count = len(far_keys) // (2 * keeps)
            specs_stay += [((count, 2 * size, quarter), FLOAT)] * keeps
            specs_go += [((count, 2 * size, quarter), SHORT)] * keeps
        weights, evidence, *sends = call(
            functools.partial(
                softmax_body, order, places, per_owner, own, leave, cut, len(partial)
            ),
            [((cut, 2 * local), SHORT), ((1, 2 * local), FLOAT)] + specs_go,
            COSTS["softmax"],
            *partial,
            *others,
            precision,
            class_id,
            place,
            where,
            particles,
            other,
            smem=(2 * len(partial) + 2, 2 * len(partial) + 3),
        )
        held, *kept = call(
            weigh_body, specs_stay, COSTS["weigh"], weights, where, particles, other, smem=(1,)
        )

        near = [swap_cls(part, k, "near") for k, part in enumerate(sends[: near_count - 1], 1)]
        ends = []
        if far_count:
            far = sends[near_count - 1 :]
            fresh = [swap_plane(far[i], steps - 1, f"far{i}") for i in range(keeps)[::-1]][::-1]
            kept = [part + new.astype(FLOAT) for part, new in zip(kept, fresh, strict=True)]
            for step in range(steps - 2, -1, -1):
                stay, send = kept
                if step == steps - 2:
                    send = send.astype(SHORT)
                if step == 0:
                    fresh = swap_plane(send, step, "far")
                    kept = [stay + fresh.astype(FLOAT)]
                    continue
                n = stay.shape[0] // 2
                away = stay[n:] + swap_plane(send[n:], step, "far1").astype(FLOAT)
                kept = [stay[:n] + swap_plane(send[:n], step, "far0").astype(FLOAT), away]
            for k in range(near_count, owners):
                j = k - near_count
                ends.append(swap_cls(kept[0][j : j + 1].astype(SHORT), k, "far"))
            ends = call(sum_body, [((1, 2 * size, quarter), FLOAT)], COSTS["sum"], *ends)
        kinds = [FLOAT] * (positions - 1) + [SHORT]
        own_parts = call(
            near_body,
            [((1, 2 * size, quarter), kind) for kind in kinds],
            COSTS["near"],
            held,
            *near,
        )
        ends = [own_parts[0], *ends]
        for q in range(positions - 1, 0, -1):
            ends.append(swap(own_parts[q], masks_of(q), f"plane_own{q}"))
        kept, sent = call(
            total_body,
            [((2, mine_rows, quarter), FLOAT)] * 2,
            (0, 8 * size * half),
            where,
            *ends,
            smem=(0,),
        )
        got = swap_core(sent, "sums")
        class_sums = call(
            final_body,
            [((per_owner, own, width), FLOAT)],
            (0, 8 * mine_rows * width),
            where,
            kept,
            got,
            smem=(0,),
        )[0]
        return class_sums, evidence[0, :local]

    return jax.shard_map(
        on_device,
        mesh=mesh,
        in_specs=(
            P(("cls", "dom"), None),
            P(("cls", "dom"), None),
            P(("cls", "dom")),
            P("cls", "dom", None),
        ),
        out_specs=(P("cls", "dom", None), P(("cls", "dom"))),
        check_vma=False,
    )
```
